128 devices in a mesh: row: 16 (over x, z), col: 8 (over y, core).
Axes of the slice: x: 4, y: 4, z: 4, core: 2. Of those that a mesh axis runs over, the one named last changes fastest.
Arguments:
- snapshots: bfloat16 [512, 524288], P(('row', 'col')), may hold values from -60 to 60, as said below
- block_order: int32 [1024], replicated, may hold values from 0 to 1023, each once
Outputs:
- scaled_factor: float32 [512, 512], replicated
- basis: float32 [512, 524288], P(None, ('row', 'col'))
The draws below stay inside these ranges and needn't reach their ends.
Inputs may be any that keep to these rules, and one draw needn't show every extreme that they name: `block_order`: every block index appears exactly once. `snapshots`: entries stay within the range.
All inputs are finite; a program needn't handle non-finite values.
Results may differ from the reference program's by a relative error of at most 0.0003.
The reference program's roundings to bfloat16 on the way (of `reordered` and `inverse`) count: a program that leaves them out, or rounds other values in their place, can miss the bound.
Values may be sent and summed in bfloat16 or wider, within the bound.
A program may use at most 128 MiB of HBM per device.

```python
import math
import jax
import jax.numpy as jnp
from jax import lax

K = 512
NBLOCKS = 1024
NROWS = 524288


def draw_snapshots(key, part):
    first, second = jax.random.split(key, 2)
    scales = jnp.exp(jax.random.uniform(first, (K, 1), jnp.float32, 0.0, math.log(10.0)))
    values = scales * jnp.clip(jax.random.normal(second, (K, NROWS), jnp.float32), -6.0, 6.0)
    return values.astype(jnp.bfloat16)


def setup_inputs(seed: int = 0) -> dict:
    seeds = jax.random.split(jax.random.key(seed), 3)
    snapshots = draw_snapshots(jax.random.fold_in(seeds[2], 71), 0)
    block_order = jax.random.permutation(seeds[1], NBLOCKS).astype(jnp.int32)
    return dict(snapshots=snapshots, block_order=block_order)


def small_pair(matrix):
    size = matrix.shape[0]
    lower = jnp.zeros((size, size), jnp.float32)
    for column in range(size):
        prior = lower[column, :column]
        pivot = jnp.sqrt(matrix[column, column] - jnp.sum(prior * prior))
        lower = lower.at[column, column].set(pivot)
        if column + 1 < size:
            below = matrix[column + 1:, column] - lax.optimization_barrier(jnp.sum(lower[column + 1:, :column] * prior[None, :], axis=1))
            lower = lower.at[column + 1:, column].set(below / pivot)
    inverse = jnp.zeros((size, size), jnp.float32)
    for line in range(size):
        unit = jnp.zeros((size,), jnp.float32).at[line].set(1.0)
        known = lax.optimization_barrier(jnp.sum(lower[line, :line][:, None] * inverse[:line, :], axis=0))
        inverse = inverse.at[line, :].set((unit - known) / lower[line, line])
    return (lower, inverse)

def factor_pair(matrix):
    size = matrix.shape[0]
    if size <= 16:
        return small_pair(matrix)
    half = size // 2
    exact = lax.Precision.HIGHEST
    lower_first, inverse_first = factor_pair(matrix[:half, :half])
    lower_cross = jnp.dot(matrix[half:, :half], inverse_first.T, precision=exact)
    trailing = matrix[half:, half:] - jnp.dot(lower_cross, lower_cross.T, precision=exact)
    lower_second, inverse_second = factor_pair(trailing)
    inverse_cross = -jnp.dot(inverse_second, jnp.dot(lower_cross, inverse_first, precision=exact), precision=exact)
    zeros_block = jnp.zeros((half, size - half), jnp.float32)
    lower = jnp.concatenate([jnp.concatenate([lower_first, zeros_block], axis=1), jnp.concatenate([lower_cross, lower_second], axis=1)], axis=0)
    inverse = jnp.concatenate([jnp.concatenate([inverse_first, zeros_block], axis=1), jnp.concatenate([inverse_cross, inverse_second], axis=1)], axis=0)
    return (lower, inverse)

def reference(snapshots, block_order):
    width = snapshots.shape[0]
    total_rows = snapshots.shape[1]
    nblocks = block_order.shape[0]
    block_rows = total_rows // nblocks
    reordered = snapshots.reshape(width, nblocks, block_rows)[:, block_order, :].reshape(width, total_rows)
    gram = jnp.dot(reordered, reordered.T, preferred_element_type=jnp.float32)
    lower, lower_inverse = factor_pair(gram)
    root = math.sqrt(total_rows)
    scaled_factor = lower.T / root
    inverse = (lower_inverse.T * root).astype(jnp.bfloat16)
    basis = jnp.dot(inverse.T, reordered, preferred_element_type=jnp.float32)
    return (scaled_factor, basis)
```

```python
import math, functools
import jax, jax.numpy as jnp
from jax import lax
from jax.experimental import pallas as pl
from jax.experimental.pallas import tpu as pltpu
from jax.sharding import PartitionSpec as P

TILE = 128
GROUP = 4
CHUNK = 512
EXACT = lax.Precision.HIGHEST


def factor_tile(work):
    lanes = lax.broadcasted_iota(jnp.int32, (8, TILE), 1)
    subs = lax.broadcasted_iota(jnp.int32, (8, TILE), 0)
    nslab = TILE // 8
    left = [work[8 * s : 8 * s + 8, :] for s in range(nslab)]
    right = [(lanes == subs + 8 * s).astype(jnp.float32) for s in range(nslab)]
    upper_rows, inverse_rows = [], []
    for start in range(0, TILE, GROUP):
        slab, base = start // 8, start % 8
        rows = [jnp.broadcast_to(left[slab][base + k : base + k + 1, :], (8, TILE)) for k in range(GROUP)]
        sides = [jnp.broadcast_to(right[slab][base + k : base + k + 1, :], (8, TILE)) for k in range(GROUP)]
        columns = [
            [jnp.broadcast_to(left[s][:, start + k : start + k + 1], (8, TILE)) for k in range(GROUP)]
            for s in range(slab, nslab)
        ]
        corner = [
            [jnp.broadcast_to(rows[k][:, start + l : start + l + 1], (8, TILE)) if l >= k else None for l in range(GROUP)]
            for k in range(GROUP)
        ]
        scales, inverses, scaled_rows, scaled_sides = [], [], [], []
        for k in range(GROUP):
            pivot = corner[k][k]
            guess = lax.rsqrt(pivot)
            root = guess * (1.5 - (0.5 * pivot) * guess * guess)
            reciprocal = root * root
            ratios = [corner[k][l] * reciprocal for l in range(k + 1, GROUP)]
            for l in range(k + 1, GROUP):
                ratio = ratios[l - k - 1]
                for m in range(l, GROUP):
                    corner[l][m] = corner[l][m] - ratio * corner[k][m]
                rows[l] = rows[l] - ratio * rows[k]
                sides[l] = sides[l] - ratio * sides[k]
                for column in columns:
                    column[l] = column[l] - ratio * column[k]
            upper_rows.append(rows[k][:1, :] * root[:1, :])
            inverse_rows.append(sides[k][:1, :] * root[:1, :])
            scaled_rows.append(rows[k] * reciprocal)
            scaled_sides.append(sides[k] * reciprocal)
        first = slab + (1 if base + GROUP == 8 else 0)
        for s in range(first, nslab):
            column = columns[s - slab]
            new_left, new_right = left[s], right[s]
            for k in range(GROUP):
                new_left = new_left - column[k] * scaled_rows[k]
                new_right = new_right - column[k] * scaled_sides[k]
            left[s], right[s] = new_left, new_right
    upper = jnp.concatenate(upper_rows, axis=0)
    inverse = jnp.concatenate(inverse_rows, axis=0)
    return upper, inverse


def mul(a, b):
    return lax.dot_general(a, b, (((1,), (0,)), ((), ())), precision=EXACT, preferred_element_type=jnp.float32)


def mul_t(a, b):
    return lax.dot_general(a, b, (((0,), (0,)), ((), ())), precision=EXACT, preferred_element_type=jnp.float32)


def factor_kernel(gram, owned_hbm, factor, basis_hbm, work, side, owned, basis, owned_sem, basis_sem, *, root):
    size, width = owned.shape
    fetch = pltpu.make_async_copy(owned_hbm, owned, owned_sem)
    fetch.start()
    work[...] = gram[...]
    panels = size // TILE
    stores = []
    for p in range(panels):
        lo, hi = p * TILE, (p + 1) * TILE
        upper, inverse = factor_tile(work[lo:hi, lo:hi])
        rows = lax.broadcasted_iota(jnp.int32, (TILE, TILE), 0)
        lanes = lax.broadcasted_iota(jnp.int32, (TILE, TILE), 1)
        factor[lo:hi, lo:hi] = jnp.where(lanes >= rows, upper, 0.0) / root
        if p:
            factor[lo:hi, :lo] = jnp.zeros((TILE, lo), jnp.float32)
            inverse = jnp.concatenate([mul(inverse, side[lo:hi, :lo]), inverse], axis=1)
        if hi < size:
            cross = mul(inverse[:, lo:hi], work[lo:hi, hi:])
            factor[lo:hi, hi:] = cross / root
            work[hi:, hi:] = work[hi:, hi:] - mul_t(cross, cross)
            update = -mul_t(cross, inverse)
            if p:
                side[hi:, :lo] = side[hi:, :lo] + update[:, :lo]
            side[hi:, lo:hi] = update[:, lo:hi]
        if p == 0:
            fetch.wait()
        narrow = (inverse * root).astype(jnp.bfloat16)

        def columns(c, carry, narrow=narrow, lo=lo, hi=hi):
            at = pl.ds(pl.multiple_of(c * CHUNK, CHUNK), CHUNK)
            basis[lo:hi, at] = jnp.dot(narrow, owned[:hi, at], preferred_element_type=jnp.float32)
            return carry

        lax.fori_loop(0, width // CHUNK, columns, 0)
        store = pltpu.make_async_copy(basis.at[lo:hi, :], basis_hbm.at[lo:hi, :], basis_sem.at[p])
        store.start()
        stores.append(store)
    for store in stores:
        store.wait()


def factor_and_basis(gram, owned, total_rows):
    size, width = owned.shape
    return pl.pallas_call(
        functools.partial(factor_kernel, root=math.sqrt(total_rows)),
        out_shape=(
            jax.ShapeDtypeStruct((size, size), jnp.float32),
            jax.ShapeDtypeStruct((size, width), jnp.float32),
        ),
        in_specs=[pl.BlockSpec(memory_space=pltpu.VMEM), pl.BlockSpec(memory_space=pl.ANY)],
        out_specs=(pl.BlockSpec(memory_space=pltpu.VMEM), pl.BlockSpec(memory_space=pl.ANY)),
        scratch_shapes=[
            pltpu.VMEM((size, size), jnp.float32),
            pltpu.VMEM((size, size), jnp.float32),
            pltpu.VMEM((size, width), jnp.bfloat16),
            pltpu.VMEM((size, width), jnp.float32),
            pltpu.SemaphoreType.DMA,
            pltpu.SemaphoreType.DMA((size // TILE,)),
        ],
        compiler_params=pltpu.CompilerParams(vmem_limit_bytes=40 * 2**20),
        name="factor_and_basis",
    )(gram, owned)


def sum_over_devices(local, devices):
    size = local.shape[0]
    share = local.reshape(devices, -1, 128)
    parts = lax.all_to_all(share, ("row", "col"), split_axis=0, concat_axis=0, tiled=True)
    total = jnp.sum(parts, axis=0)
    spread = jnp.broadcast_to(total[None], parts.shape)
    whole = lax.all_to_all(spread, ("row", "col"), split_axis=0, concat_axis=0, tiled=True)
    return whole.reshape(size, size)


def per_device(snapshots, block_order, devices):
    local_count = snapshots.shape[0]
    total_rows = snapshots.shape[1]
    nblocks = block_order.shape[0]
    block_rows = total_rows // nblocks
    reordered = snapshots.reshape(local_count, nblocks, block_rows)[:, block_order, :].reshape(
        local_count, total_rows
    )
    owned = lax.all_to_all(reordered, ("row", "col"), split_axis=1, concat_axis=0, tiled=True)
    gram = jnp.dot(owned, owned.T, preferred_element_type=jnp.float32)
    summed = sum_over_devices(gram, devices)
    return factor_and_basis(summed, owned, total_rows)


def solution(mesh):
    placed = (P(("row", "col"), None), P())
    return jax.shard_map(
        functools.partial(per_device, devices=mesh.size),
        mesh=mesh,
        in_specs=placed,
        out_specs=(P(), P(None, ("row", "col"))),
        check_vma=False,
    )
```

```python
import math, functools
import jax, jax.numpy as jnp
from jax import lax
from jax.experimental import pallas as pl
from jax.experimental.pallas import tpu as pltpu
from jax.sharding import PartitionSpec as P

TILE = 128
GROUP = 4
CHUNK = 512
VMEM_BYTES = 56 * 2**20
MESH = pl.DeviceIdType.MESH
EXACT = lax.Precision.HIGHEST


def factor_tile(work):
    lanes = lax.broadcasted_iota(jnp.int32, (8, TILE), 1)
    subs = lax.broadcasted_iota(jnp.int32, (8, TILE), 0)
    nslab = TILE // 8
    left = [work[8 * s : 8 * s + 8, :] for s in range(nslab)]
    right = [(lanes == subs + 8 * s).astype(jnp.float32) for s in range(nslab)]
    upper_rows, inverse_rows = [], []
    for start in range(0, TILE, GROUP):
        slab, base = start // 8, start % 8
        rows = [jnp.broadcast_to(left[slab][base + k : base + k + 1, :], (8, TILE)) for k in range(GROUP)]
        sides = [jnp.broadcast_to(right[slab][base + k : base + k + 1, :], (8, TILE)) for k in range(GROUP)]
        columns = [
            [jnp.broadcast_to(left[s][:, start + k : start + k + 1], (8, TILE)) for k in range(GROUP)]
            for s in range(slab, nslab)
        ]
        corner = [
            [jnp.broadcast_to(rows[k][:, start + l : start + l + 1], (8, TILE)) if l >= k else None for l in range(GROUP)]
            for k in range(GROUP)
        ]
        scales, inverses, scaled_rows, scaled_sides = [], [], [], []
        for k in range(GROUP):
            pivot = corner[k][k]
            guess = lax.rsqrt(pivot)
            root = guess * (1.5 - (0.5 * pivot) * guess * guess)
            reciprocal = root * root
            ratios = [corner[k][l] * reciprocal for l in range(k + 1, GROUP)]
            for l in range(k + 1, GROUP):
                ratio = ratios[l - k - 1]
                for m in range(l, GROUP):
                    corner[l][m] = corner[l][m] - ratio * corner[k][m]
                rows[l] = rows[l] - ratio * rows[k]
                sides[l] = sides[l] - ratio * sides[k]
                for column in columns:
                    column[l] = column[l] - ratio * column[k]
            upper_rows.append(rows[k][:1, :] * root[:1, :])
            inverse_rows.append(sides[k][:1, :] * root[:1, :])
            scaled_rows.append(rows[k] * reciprocal)
            scaled_sides.append(sides[k] * reciprocal)
        first = slab + (1 if base + GROUP == 8 else 0)
        for s in range(first, nslab):
            column = columns[s - slab]
            new_left, new_right = left[s], right[s]
            for k in range(GROUP):
                new_left = new_left - column[k] * scaled_rows[k]
                new_right = new_right - column[k] * scaled_sides[k]
            left[s], right[s] = new_left, new_right
    upper = jnp.concatenate(upper_rows, axis=0)
    inverse = jnp.concatenate(inverse_rows, axis=0)
    return upper, inverse


def mul(a, b):
    return lax.dot_general(a, b, (((1,), (0,)), ((), ())), precision=EXACT, preferred_element_type=jnp.float32)


def mul_t(a, b):
    return lax.dot_general(a, b, (((0,), (0,)), ((), ())), precision=EXACT, preferred_element_type=jnp.float32)


def factor_kernel(gram, owned_hbm, factor, basis_hbm, work, side, owned, basis, owned_sem, basis_sem, *, root):
    size, width = owned.shape
    fetch = pltpu.make_async_copy(owned_hbm, owned, owned_sem)
    fetch.start()
    work[...] = gram[...]
    panels = size // TILE
    stores = []
    for p in range(panels):
        lo, hi = p * TILE, (p + 1) * TILE
        upper, inverse = factor_tile(work[lo:hi, lo:hi])
        rows = lax.broadcasted_iota(jnp.int32, (TILE, TILE), 0)
        lanes = lax.broadcasted_iota(jnp.int32, (TILE, TILE), 1)
        factor[lo:hi, lo:hi] = jnp.where(lanes >= rows, upper, 0.0) / root
        if p:
            factor[lo:hi, :lo] = jnp.zeros((TILE, lo), jnp.float32)
            inverse = jnp.concatenate([mul(inverse, side[lo:hi, :lo]), inverse], axis=1)
        if hi < size:
            cross = mul(inverse[:, lo:hi], work[lo:hi, hi:])
            factor[lo:hi, hi:] = cross / root
            work[hi:, hi:] = work[hi:, hi:] - mul_t(cross, cross)
            update = -mul_t(cross, inverse)
            if p:
                side[hi:, :lo] = side[hi:, :lo] + update[:, :lo]
            side[hi:, lo:hi] = update[:, lo:hi]
        if p == 0:
            fetch.wait()
        narrow = (inverse * root).astype(jnp.bfloat16)

        def columns(c, carry, narrow=narrow, lo=lo, hi=hi):
            at = pl.ds(pl.multiple_of(c * CHUNK, CHUNK), CHUNK)
            basis[lo:hi, at] = jnp.dot(narrow, owned[:hi, at], preferred_element_type=jnp.float32)
            return carry

        lax.fori_loop(0, width // CHUNK, columns, 0)
        store = pltpu.make_async_copy(basis.at[lo:hi, :], basis_hbm.at[lo:hi, :], basis_sem.at[p])
        store.start()
        stores.append(store)
    for store in stores:
        store.wait()


def factor_and_basis(gram, owned, total_rows):
    size, width = owned.shape
    return pl.pallas_call(
        functools.partial(factor_kernel, root=math.sqrt(total_rows)),
        out_shape=(
            jax.ShapeDtypeStruct((size, size), jnp.float32),
            jax.ShapeDtypeStruct((size, width), jnp.float32),
        ),
        in_specs=[pl.BlockSpec(memory_space=pltpu.VMEM), pl.BlockSpec(memory_space=pl.ANY)],
        out_specs=(pl.BlockSpec(memory_space=pltpu.VMEM), pl.BlockSpec(memory_space=pl.ANY)),
        scratch_shapes=[
            pltpu.VMEM((size, size), jnp.float32),
            pltpu.VMEM((size, size), jnp.float32),
            pltpu.VMEM((size, width), jnp.bfloat16),
            pltpu.VMEM((size, width), jnp.float32),
            pltpu.SemaphoreType.DMA,
            pltpu.SemaphoreType.DMA((size // TILE,)),
        ],
        compiler_params=pltpu.CompilerParams(vmem_limit_bytes=VMEM_BYTES),
        name="factor_and_basis",
    )(gram, owned)


def position():
    row, col = lax.axis_index("row"), lax.axis_index("col")
    x, y = lax.div(row, 4), lax.div(col, 2)
    return row, col, x, row - 4 * x, y, col - 2 * y


def wrap(place):
    return jnp.where(place >= 4, place - 4, place)


def each_partner(place, both, visit):
    row, col, x, z, y, core = place
    ring = [y] + [wrap(y + d) for d in range(1, 4)]
    cores = [core, 1 - core] if both else [core]

    def turn(step, carry):
        outer = lax.div(step, 4)
        from_x, from_z = wrap(x + outer), wrap(z + step - 4 * outer)
        for d in range(4):
            there_row = wrap(from_x + d) * 4 + wrap(from_z + (4 - d) % 4)
            for c, there_core in enumerate(cores):
                there = (there_row, ring[d] * 2 + there_core)
                if d or c:
                    visit(there)
                else:
                    pl.when(step > 0)(functools.partial(visit, there))
        return carry

    lax.fori_loop(0, 16, turn, 0)


def exchange_kernel(order, snapshots_hbm, arrived, snapshots, staged, fetch_sem, own_sem, send_sem, recv_sem):
    place = position()
    count, _, width = staged.shape
    mine = place[0] * 8 + place[1]
    block = snapshots.shape[2]
    each = width // block
    fetch = pltpu.make_async_copy(snapshots_hbm, snapshots, fetch_sem)
    fetch.start()
    barrier = pltpu.get_barrier_semaphore()

    def greet(there):
        pl.semaphore_signal(barrier, inc=1, device_id=there, device_id_type=MESH)

    each_partner(place, True, greet)
    fetch.wait()

    def gather(there, carry):
        for k in range(each):
            staged[there, :, k * block : (k + 1) * block] = snapshots[order[there * each + k]]
        return carry

    lax.fori_loop(0, count, gather, 0)
    pl.semaphore_wait(barrier, count - 1)

    def send(there):
        pltpu.make_async_remote_copy(
            src_ref=staged.at[there[0] * 8 + there[1]],
            dst_ref=arrived.at[mine],
            send_sem=send_sem,
            recv_sem=recv_sem,
            device_id=there,
            device_id_type=MESH,
        ).start()

    each_partner(place, True, send)
    own = pltpu.make_async_copy(staged.at[mine], arrived.at[mine], own_sem)
    own.start()
    own.wait()
    others = staged.at[pl.ds(0, count - 1)]
    pltpu.make_async_copy(others, others, send_sem).wait()
    pltpu.make_async_copy(others, others, recv_sem).wait()


def exchange(snapshots, block_order, devices):
    nblocks, local_count, block_rows = snapshots.shape
    shape = (devices, local_count, nblocks * block_rows // devices)
    return pl.pallas_call(
        exchange_kernel,
        out_shape=jax.ShapeDtypeStruct(shape, snapshots.dtype),
        in_specs=[pl.BlockSpec(memory_space=pltpu.SMEM), pl.BlockSpec(memory_space=pl.ANY)],
        out_specs=pl.BlockSpec(memory_space=pl.ANY),
        scratch_shapes=[
            pltpu.VMEM(snapshots.shape, snapshots.dtype),
            pltpu.VMEM(shape, snapshots.dtype),
            pltpu.SemaphoreType.DMA,
            pltpu.SemaphoreType.DMA,
            pltpu.SemaphoreType.DMA,
            pltpu.SemaphoreType.DMA,
        ],
        compiler_params=pltpu.CompilerParams(
            collective_id=0, has_side_effects=True, vmem_limit_bytes=VMEM_BYTES
        ),
        name="exchange",
    )(block_order, snapshots)


def gram_kernel(arrived, owned, gram):
    step = pl.program_id(0)
    count, depth, width = arrived.shape
    block = arrived[...].reshape(count * depth, width)
    owned[...] = block
    part = lax.dot_general(block, block, (((1,), (1,)), ((), ())), preferred_element_type=jnp.float32)

    @pl.when(step == 0)
    def _():
        gram[...] = part

    @pl.when(step > 0)
    def _():
        gram[...] = gram[...] + part


def local_gram(arrived):
    count, depth, width = arrived.shape
    size = count * depth
    return pl.pallas_call(
        gram_kernel,
        grid=(width // CHUNK,),
        out_shape=(
            jax.ShapeDtypeStruct((size, width), arrived.dtype),
            jax.ShapeDtypeStruct((size, size), jnp.float32),
        ),
        in_specs=[pl.BlockSpec((count, depth, CHUNK), lambda s: (0, 0, s))],
        out_specs=(pl.BlockSpec((size, CHUNK), lambda s: (0, s)), pl.BlockSpec((size, size), lambda s: (0, 0))),
        compiler_params=pltpu.CompilerParams(vmem_limit_bytes=VMEM_BYTES),
        name="local_gram",
    )(arrived)


def sum_kernel(gram, total, half, parts, part, pair_send, pair_recv, send_sem, recv_sem, back_send, back_recv, last_send, last_recv):
    place = position()
    row, col, x, z, y, core = place
    size = gram.shape[0]
    middle = size // 2
    chips = parts.shape[0]
    sibling = (row, 2 * y + 1 - core)
    chip = row * 4 + y

    barrier = pltpu.get_barrier_semaphore()

    def greet(there):
        pl.semaphore_signal(barrier, inc=1, device_id=there, device_id_type=MESH)

    greet(sibling)
    each_partner(place, False, greet)
    pl.semaphore_wait(barrier, chips)

    mine = pl.multiple_of(core * middle, middle)
    theirs = pl.multiple_of((1 - core) * middle, middle)
    pair = pltpu.make_async_remote_copy(
        src_ref=gram.at[pl.ds(theirs, middle)],
        dst_ref=half,
        send_sem=pair_send,
        recv_sem=pair_recv,
        device_id=sibling,
        device_id_type=MESH,
    )
    pair.start()
    pair.wait()
    half[...] = half[...] + gram[pl.ds(mine, middle), :]

    def send(there):
        top, left = pl.multiple_of(there[0] * 16, 16), pl.multiple_of((there[1] - core) * 64, 128)
        pltpu.make_async_remote_copy(
            src_ref=half.at[pl.ds(top, 16), pl.ds(left, 128)],
            dst_ref=parts.at[chip],
            send_sem=send_sem,
            recv_sem=recv_sem,
            device_id=there,
            device_id_type=MESH,
        ).start()

    each_partner(place, False, send)
    top, left = pl.multiple_of(row * 16, 16), pl.multiple_of(y * 128, 128)
    parts[chip] = half[pl.ds(top, 16), pl.ds(left, 128)]
    others = parts.at[pl.ds(0, chips - 1)]
    pltpu.make_async_copy(others, others, send_sem).wait()
    pltpu.make_async_copy(others, others, recv_sem).wait()
    sum_parts = parts[0]
    for k in range(1, chips):
        sum_parts = sum_parts + parts[k]
    part[...] = sum_parts
    total[pl.ds(mine + top, 16), pl.ds(left, 128)] = sum_parts

    def back(there):
        pltpu.make_async_remote_copy(
            src_ref=part,
            dst_ref=total.at[pl.ds(mine + top, 16), pl.ds(left, 128)],
            send_sem=back_send,
            recv_sem=back_recv,
            device_id=there,
            device_id_type=MESH,
        ).start()

    each_partner(place, False, back)
    pltpu.make_async_copy(others, others, back_send).wait()
    pltpu.make_async_copy(others, others, back_recv).wait()
    last = pltpu.make_async_remote_copy(
        src_ref=total.at[pl.ds(mine, middle)],
        dst_ref=total.at[pl.ds(mine, middle)],
        send_sem=last_send,
        recv_sem=last_recv,
        device_id=sibling,
        device_id_type=MESH,
    )
    last.start()
    last.wait()


def sum_over_devices(gram, devices):
    size = gram.shape[0]
    chips = devices // 2
    return pl.pallas_call(
        sum_kernel,
        out_shape=jax.ShapeDtypeStruct(gram.shape, gram.dtype),
        in_specs=[pl.BlockSpec(memory_space=pltpu.VMEM)],
        out_specs=pl.BlockSpec(memory_space=pltpu.VMEM),
        scratch_shapes=[
            pltpu.VMEM((size // 2, size), gram.dtype),
            pltpu.VMEM((chips, 16, 128), gram.dtype),
            pltpu.VMEM((16, 128), gram.dtype),
        ]
        + [pltpu.SemaphoreType.DMA] * 8,
        compiler_params=pltpu.CompilerParams(
            collective_id=1, has_side_effects=True, vmem_limit_bytes=VMEM_BYTES
        ),
        name="sum_over_devices",
    )(gram)


def per_device(snapshots, block_order, devices):
    local_count, total_rows = snapshots.shape
    nblocks = block_order.shape[0]
    blocks = snapshots.reshape(local_count, nblocks, total_rows // nblocks).transpose(1, 0, 2)
    arrived = exchange(blocks, block_order, devices)
    owned, gram = local_gram(arrived)
    summed = sum_over_devices(gram, devices)
    return factor_and_basis(summed, owned, total_rows)


def solution(mesh):
    placed = (P(("row", "col"), None), P())
    return jax.shard_map(
        functools.partial(per_device, devices=mesh.size),
        mesh=mesh,
        in_specs=placed,
        out_specs=(P(), P(None, ("row", "col"))),
        check_vma=False,
    )
```

```python
import math, functools
import jax, jax.numpy as jnp
from jax import lax
from jax.experimental import pallas as pl
from jax.experimental.pallas import tpu as pltpu
from jax.sharding import PartitionSpec as P

TILE = 128
GROUP = 8
CHUNK = 1024
HALVES = 2
VMEM_BYTES = 56 * 2**20
MESH = pl.DeviceIdType.MESH
EXACT = lax.Precision.HIGHEST


def factor_tile(work):
    lanes = lax.broadcasted_iota(jnp.int32, (8, TILE), 1)
    subs = lax.broadcasted_iota(jnp.int32, (8, TILE), 0)
    nslab = TILE // 8
    left = [work[8 * s : 8 * s + 8, :] for s in range(nslab)]
    right = [(lanes == subs + 8 * s).astype(jnp.float32) for s in range(nslab)]
    upper_rows, inverse_rows = [], []
    for start in range(0, TILE, GROUP):
        slab, base = start // 8, start % 8
        rows = [jnp.broadcast_to(left[slab][base + k : base + k + 1, :], (8, TILE)) for k in range(GROUP)]
        sides = [jnp.broadcast_to(right[slab][base + k : base + k + 1, :], (8, TILE)) for k in range(GROUP)]
        columns = [
            [jnp.broadcast_to(left[s][:, start + k : start + k + 1], (8, TILE)) for k in range(GROUP)]
            for s in range(slab, nslab)
        ]
        corner = [
            [jnp.broadcast_to(rows[k][:, start + l : start + l + 1], (8, TILE)) if l >= k else None for l in range(GROUP)]
            for k in range(GROUP)
        ]
        for k in range(GROUP):
            root = lax.rsqrt(corner[k][k])
            rows[k] = rows[k] * root
            sides[k] = sides[k] * root
            for column in columns:
                column[k] = column[k] * root
            scaled = [corner[k][l] * root if l > k else None for l in range(GROUP)]
            for l in range(k + 1, GROUP):
                for m in range(l, GROUP):
                    corner[l][m] = corner[l][m] - scaled[l] * scaled[m]
                rows[l] = rows[l] - scaled[l] * rows[k]
                sides[l] = sides[l] - scaled[l] * sides[k]
                for column in columns:
                    column[l] = column[l] - scaled[l] * column[k]
            upper_rows.append(rows[k][:1, :])
            inverse_rows.append(sides[k][:1, :])
        first = slab + (1 if base + GROUP == 8 else 0)
        for s in range(first, nslab):
            column = columns[s - slab]
            new_left, new_right = left[s], right[s]
            for k in range(GROUP):
                new_left = new_left - column[k] * rows[k]
                new_right = new_right - column[k] * sides[k]
            left[s], right[s] = new_left, new_right
    upper = jnp.concatenate(upper_rows, axis=0)
    inverse = jnp.concatenate(inverse_rows, axis=0)
    return upper, inverse


def mul(a, b):
    return lax.dot_general(a, b, (((1,), (0,)), ((), ())), precision=EXACT, preferred_element_type=jnp.float32)


def mul_t(a, b):
    return lax.dot_general(a, b, (((0,), (0,)), ((), ())), precision=EXACT, preferred_element_type=jnp.float32)


def factor_kernel(gram, owned_hbm, factor, basis_hbm, work, side, narrow, owned, basis, owned_sem, basis_sem, *, root):
    size, width = owned.shape
    fetch = pltpu.make_async_copy(owned_hbm, owned, owned_sem)
    fetch.start()
    work[...] = gram[...]
    panels = size // TILE
    stores = []
    for p in range(panels):
        lo, hi = p * TILE, (p + 1) * TILE
        upper, inverse = factor_tile(work[lo:hi, lo:hi])
        rows = lax.broadcasted_iota(jnp.int32, (TILE, TILE), 0)
        lanes = lax.broadcasted_iota(jnp.int32, (TILE, TILE), 1)
        factor[lo:hi, lo:hi] = jnp.where(lanes >= rows, upper, 0.0) / root
        if p:
            factor[lo:hi, :lo] = jnp.zeros((TILE, lo), jnp.float32)
            inverse = jnp.concatenate([mul(inverse, side[lo:hi, :lo]), inverse], axis=1)
        if hi < size:
            cross = mul(inverse[:, lo:hi], work[lo:hi, hi:])
            factor[lo:hi, hi:] = cross / root
            work[hi:, hi:] = work[hi:, hi:] - mul_t(cross, cross)
            update = -mul_t(cross, inverse)
            if p:
                side[hi:, :lo] = side[hi:, :lo] + update[:, :lo]
            side[hi:, lo:hi] = update[:, lo:hi]
        narrow[lo:hi, :hi] = (inverse * root).astype(jnp.bfloat16)
        if hi < size:
            narrow[lo:hi, hi:] = jnp.zeros((TILE, size - hi), jnp.bfloat16)
        if p == 1:
            fetch.wait()
        if p % 2:
            first, parts = lo - TILE, 1 if hi < size else 4
            for c in range(parts):
                span = width // parts

                def columns(i, carry, first=first, hi=hi, start=c * span):
                    at = pl.ds(pl.multiple_of(start + i * CHUNK, CHUNK), CHUNK)
                    basis[first:hi, at] = jnp.dot(
                        narrow[first:hi, :hi], owned[:hi, at], preferred_element_type=jnp.float32
                    )
                    return carry

                lax.fori_loop(0, span // CHUNK, columns, 0)
                at = slice(c * span, (c + 1) * span)
                store = pltpu.make_async_copy(
                    basis.at[first:hi, at], basis_hbm.at[first:hi, at], basis_sem.at[len(stores)]
                )
                store.start()
                stores.append(store)
    for store in stores:
        store.wait()


def factor_and_basis(gram, owned, total_rows):
    size, width = owned.shape
    return pl.pallas_call(
        functools.partial(factor_kernel, root=math.sqrt(total_rows)),
        out_shape=(
            jax.ShapeDtypeStruct((size, size), jnp.float32),
            jax.ShapeDtypeStruct((size, width), jnp.float32),
        ),
        in_specs=[pl.BlockSpec(memory_space=pltpu.VMEM), pl.BlockSpec(memory_space=pl.ANY)],
        out_specs=(pl.BlockSpec(memory_space=pltpu.VMEM), pl.BlockSpec(memory_space=pl.ANY)),
        scratch_shapes=[
            pltpu.VMEM((size, size), jnp.float32),
            pltpu.VMEM((size, size), jnp.float32),
            pltpu.VMEM((size, size), jnp.bfloat16),
            pltpu.VMEM((size, width), jnp.bfloat16),
            pltpu.VMEM((size, width), jnp.float32),
            pltpu.SemaphoreType.DMA,
            pltpu.SemaphoreType.DMA((8,)),
        ],
        compiler_params=pltpu.CompilerParams(vmem_limit_bytes=VMEM_BYTES),
        name="factor_and_basis",
    )(gram, owned)


def position():
    row, col = lax.axis_index("row"), lax.axis_index("col")
    x, y = lax.div(row, 4), lax.div(col, 2)
    return row, col, x, row - 4 * x, y, col - 2 * y


def wrap(place):
    return jnp.where(place >= 4, place - 4, place)


def each_partner(place, both, visit):
    row, col, x, z, y, core = place
    ring = [y] + [wrap(y + d) for d in range(1, 4)]
    cores = [core, 1 - core] if both else [core]

    def turn(step, carry):
        outer = lax.div(step, 4)
        from_x, from_z = wrap(x + outer), wrap(z + step - 4 * outer)
        for d in range(4):
            there_row = wrap(from_x + d) * 4 + wrap(from_z + (4 - d) % 4)
            for c, there_core in enumerate(cores):
                there = (there_row, ring[d] * 2 + there_core)
                if d or c:
                    visit(there)
                else:
                    pl.when(step > 0)(functools.partial(visit, there))
        return carry

    lax.fori_loop(0, 16, turn, 0)


def exchange_kernel(
    order, snapshots_hbm, owned_hbm, total,
    snapshots, staged, arrived, owned, gram, half, parts, part,
    fetch_sem, own_sem, store_sem, block_send, block_recv,
    pair_send, pair_recv, send_sem, recv_sem, back_send, back_recv, last_send, last_recv,
):
    place = position()
    row, col, x, z, y, core = place
    pieces, count, depth, span = staged.shape
    me = row * 8 + col
    block = snapshots.shape[2]
    each = span // block
    size = gram.shape[0]
    middle = size // 2
    chips = parts.shape[0]
    sibling = (row, 2 * y + 1 - core)
    chip = row * 4 + y

    fetch = pltpu.make_async_copy(snapshots_hbm, snapshots, fetch_sem)
    fetch.start()
    barrier = pltpu.get_barrier_semaphore()

    def greet(there):
        pl.semaphore_signal(barrier, inc=1, device_id=there, device_id_type=MESH)

    each_partner(place, True, greet)
    fetch.wait()
    own = []
    for piece in range(pieces):

        def gather(there, carry, piece=piece):
            for k in range(each):
                staged[piece, there, :, k * block : (k + 1) * block] = snapshots[
                    order[(there * pieces + piece) * each + k]
                ]
            return carry

        lax.fori_loop(0, count, gather, 0)
        if piece == 0:
            pl.semaphore_wait(barrier, count - 1)

        def send_block(there, piece=piece):
            pltpu.make_async_remote_copy(
                src_ref=staged.at[piece, there[0] * 8 + there[1]],
                dst_ref=arrived.at[piece, me],
                send_sem=block_send.at[piece],
                recv_sem=block_recv.at[piece],
                device_id=there,
                device_id_type=MESH,
            ).start()

        each_partner(place, True, send_block)
        copy = pltpu.make_async_copy(staged.at[piece, me], arrived.at[piece, me], own_sem.at[piece])
        copy.start()
        own.append(copy)

    stores = []
    for piece in range(pieces):
        own[piece].wait()
        blocks = staged.at[piece, pl.ds(0, count - 1)]
        pltpu.make_async_copy(blocks, blocks, block_recv.at[piece]).wait()
        for c in range(span // CHUNK):
            got = arrived[piece, :, :, c * CHUNK : (c + 1) * CHUNK].reshape(size, CHUNK)
            owned[:, piece * span + c * CHUNK : piece * span + (c + 1) * CHUNK] = got
            product = lax.dot_general(
                got, got, (((1,), (1,)), ((), ())), preferred_element_type=jnp.float32
            )
            gram[...] = product if piece == 0 and c == 0 else gram[...] + product
        at = slice(piece * span, (piece + 1) * span)
        store = pltpu.make_async_copy(owned.at[:, at], owned_hbm.at[:, at], store_sem.at[piece])
        store.start()
        stores.append(store)

    mine = pl.multiple_of(core * middle, middle)
    theirs = pl.multiple_of((1 - core) * middle, middle)
    pair = pltpu.make_async_remote_copy(
        src_ref=gram.at[pl.ds(theirs, middle)],
        dst_ref=half,
        send_sem=pair_send,
        recv_sem=pair_recv,
        device_id=sibling,
        device_id_type=MESH,
    )
    pair.start()
    pair.wait()
    half[...] = half[...] + gram[pl.ds(mine, middle), :]

    def send(there):
        top, left = pl.multiple_of(there[0] * 16, 16), pl.multiple_of((there[1] - core) * 64, 128)
        pltpu.make_async_remote_copy(
            src_ref=half.at[pl.ds(top, 16), pl.ds(left, 128)],
            dst_ref=parts.at[chip],
            send_sem=send_sem,
            recv_sem=recv_sem,
            device_id=there,
            device_id_type=MESH,
        ).start()

    each_partner(place, False, send)
    top, left = pl.multiple_of(row * 16, 16), pl.multiple_of(y * 128, 128)
    parts[chip] = half[pl.ds(top, 16), pl.ds(left, 128)]
    others = parts.at[pl.ds(0, chips - 1)]
    pltpu.make_async_copy(others, others, send_sem).wait()
    pltpu.make_async_copy(others, others, recv_sem).wait()
    sum_parts = parts[0]
    for k in range(1, chips):
        sum_parts = sum_parts + parts[k]
    part[...] = sum_parts
    total[pl.ds(mine + top, 16), pl.ds(left, 128)] = sum_parts

    def back(there):
        pltpu.make_async_remote_copy(
            src_ref=part,
            dst_ref=total.at[pl.ds(mine + top, 16), pl.ds(left, 128)],
            send_sem=back_send,
            recv_sem=back_recv,
            device_id=there,
            device_id_type=MESH,
        ).start()

    each_partner(place, False, back)
    pltpu.make_async_copy(others, others, back_send).wait()
    pltpu.make_async_copy(others, others, back_recv).wait()
    last = pltpu.make_async_remote_copy(
        src_ref=total.at[pl.ds(mine, middle)],
        dst_ref=total.at[pl.ds(mine, middle)],
        send_sem=last_send,
        recv_sem=last_recv,
        device_id=sibling,
        device_id_type=MESH,
    )
    last.start()
    last.wait()
    for piece in range(pieces):
        blocks = staged.at[piece, pl.ds(0, count - 1)]
        pltpu.make_async_copy(blocks, blocks, block_send.at[piece]).wait()
        stores[piece].wait()


def exchange(snapshots, block_order, devices):
    nblocks, local_count, block_rows = snapshots.shape
    size, width = devices * local_count, nblocks * block_rows // devices
    chips = devices // 2
    landing = pltpu.VMEM((HALVES, devices, local_count, width // HALVES), snapshots.dtype)
    return pl.pallas_call(
        exchange_kernel,
        out_shape=(
            jax.ShapeDtypeStruct((size, width), snapshots.dtype),
            jax.ShapeDtypeStruct((size, size), jnp.float32),
        ),
        in_specs=[pl.BlockSpec(memory_space=pltpu.SMEM), pl.BlockSpec(memory_space=pl.ANY)],
        out_specs=(pl.BlockSpec(memory_space=pl.ANY), pl.BlockSpec(memory_space=pltpu.VMEM)),
        scratch_shapes=[
            pltpu.VMEM(snapshots.shape, snapshots.dtype),
            landing,
            landing,
            pltpu.VMEM((size, width), snapshots.dtype),
            pltpu.VMEM((size, size), jnp.float32),
            pltpu.VMEM((size // 2, size), jnp.float32),
            pltpu.VMEM((chips, 16, 128), jnp.float32),
            pltpu.VMEM((16, 128), jnp.float32),
            pltpu.SemaphoreType.DMA,
            pltpu.SemaphoreType.DMA((HALVES,)),
            pltpu.SemaphoreType.DMA((HALVES,)),
            pltpu.SemaphoreType.DMA((HALVES,)),
            pltpu.SemaphoreType.DMA((HALVES,)),
        ]
        + [pltpu.SemaphoreType.DMA] * 8,
        compiler_params=pltpu.CompilerParams(
            collective_id=0, has_side_effects=True, vmem_limit_bytes=VMEM_BYTES
        ),
        name="exchange",
    )(block_order, snapshots)


def per_device(snapshots, block_order, devices):
    local_count, total_rows = snapshots.shape
    nblocks = block_order.shape[0]
    blocks = snapshots.reshape(local_count, nblocks, total_rows // nblocks).transpose(1, 0, 2)
    owned, summed = exchange(blocks, block_order, devices)
    return factor_and_basis(summed, owned, total_rows)


def solution(mesh):
    placed = (P(("row", "col"), None), P())
    return jax.shard_map(
        functools.partial(per_device, devices=mesh.size),
        mesh=mesh,
        in_specs=placed,
        out_specs=(P(), P(None, ("row", "col"))),
        check_vma=False,
    )
```

```python
import math, functools
import jax, jax.numpy as jnp
from jax import lax
from jax.experimental import pallas as pl
from jax.experimental.pallas import tpu as pltpu
from jax.sharding import PartitionSpec as P

TILE = 128
GROUP = 8
CHUNK = 1024
HALVES = 2
VMEM_BYTES = 56 * 2**20
MESH = pl.DeviceIdType.MESH
EXACT = lax.Precision.HIGHEST


def factor_tile(work):
    lanes = lax.broadcasted_iota(jnp.int32, (8, TILE), 1)
    subs = lax.broadcasted_iota(jnp.int32, (8, TILE), 0)
    nslab = TILE // 8
    left = [work[8 * s : 8 * s + 8, :] for s in range(nslab)]
    right = [(lanes == subs + 8 * s).astype(jnp.float32) for s in range(nslab)]
    upper_rows, inverse_rows = [], []
    for start in range(0, TILE, GROUP):
        slab, base = start // 8, start % 8
        rows = [jnp.broadcast_to(left[slab][base + k : base + k + 1, :], (8, TILE)) for k in range(GROUP)]
        sides = [jnp.broadcast_to(right[slab][base + k : base + k + 1, :], (8, TILE)) for k in range(GROUP)]
        columns = [
            [jnp.broadcast_to(left[s][:, start + k : start + k + 1], (8, TILE)) for k in range(GROUP)]
            for s in range(slab, nslab)
        ]
        corner = [
            [jnp.broadcast_to(rows[k][:, start + l : start + l + 1], (8, TILE)) if l >= k else None for l in range(GROUP)]
            for k in range(GROUP)
        ]
        for k in range(GROUP):
            root = lax.rsqrt(corner[k][k])
            rows[k] = rows[k] * root
            sides[k] = sides[k] * root
            for column in columns:
                column[k] = column[k] * root
            scaled = [corner[k][l] * root if l > k else None for l in range(GROUP)]
            for l in range(k + 1, GROUP):
                for m in range(l, GROUP):
                    corner[l][m] = corner[l][m] - scaled[l] * scaled[m]
                rows[l] = rows[l] - scaled[l] * rows[k]
                sides[l] = sides[l] - scaled[l] * sides[k]
                for column in columns:
                    column[l] = column[l] - scaled[l] * column[k]
            upper_rows.append(rows[k][:1, :])
            inverse_rows.append(sides[k][:1, :])
        first = slab + (1 if base + GROUP == 8 else 0)
        for s in range(first, nslab):
            column = columns[s - slab]
            new_left, new_right = left[s], right[s]
            for k in range(GROUP):
                new_left = new_left - column[k] * rows[k]
                new_right = new_right - column[k] * sides[k]
            left[s], right[s] = new_left, new_right
    upper = jnp.concatenate(upper_rows, axis=0)
    inverse = jnp.concatenate(inverse_rows, axis=0)
    return upper, inverse


def mul(a, b):
    return lax.dot_general(a, b, (((1,), (0,)), ((), ())), precision=EXACT, preferred_element_type=jnp.float32)


def mul_t(a, b):
    return lax.dot_general(a, b, (((0,), (0,)), ((), ())), precision=EXACT, preferred_element_type=jnp.float32)


def factor_kernel(gram, owned_hbm, factor, basis_hbm, work, side, narrow, owned, basis, owned_sem, basis_sem, *, root):
    size, width = owned.shape
    fetch = pltpu.make_async_copy(owned_hbm, owned, owned_sem)
    fetch.start()
    work[...] = gram[...]
    panels = size // TILE
    stores = []
    for p in range(panels):
        lo, hi = p * TILE, (p + 1) * TILE
        upper, inverse = factor_tile(work[lo:hi, lo:hi])
        rows = lax.broadcasted_iota(jnp.int32, (TILE, TILE), 0)
        lanes = lax.broadcasted_iota(jnp.int32, (TILE, TILE), 1)
        factor[lo:hi, lo:hi] = jnp.where(lanes >= rows, upper, 0.0) / root
        if p:
            factor[lo:hi, :lo] = jnp.zeros((TILE, lo), jnp.float32)
            inverse = jnp.concatenate([mul(inverse, side[lo:hi, :lo]), inverse], axis=1)
        if hi < size:
            cross = mul(inverse[:, lo:hi], work[lo:hi, hi:])
            factor[lo:hi, hi:] = cross / root
            work[hi:, hi:] = work[hi:, hi:] - mul_t(cross, cross)
            update = -mul_t(cross, inverse)
            if p:
                side[hi:, :lo] = side[hi:, :lo] + update[:, :lo]
            side[hi:, lo:hi] = update[:, lo:hi]
        narrow[lo:hi, :hi] = (inverse * root).astype(jnp.bfloat16)
        if hi < size:
            narrow[lo:hi, hi:] = jnp.zeros((TILE, size - hi), jnp.bfloat16)
        if p == 1:
            fetch.wait()
        if p % 2:
            first, parts = lo - TILE, 1 if hi < size else 4
            for c in range(parts):
                span = width // parts

                def columns(i, carry, first=first, hi=hi, start=c * span):
                    at = pl.ds(pl.multiple_of(start + i * CHUNK, CHUNK), CHUNK)
                    basis[first:hi, at] = jnp.dot(
                        narrow[first:hi, :hi], owned[:hi, at], preferred_element_type=jnp.float32
                    )
                    return carry

                lax.fori_loop(0, span // CHUNK, columns, 0)
                at = slice(c * span, (c + 1) * span)
                store = pltpu.make_async_copy(
                    basis.at[first:hi, at], basis_hbm.at[first:hi, at], basis_sem.at[len(stores)]
                )
                store.start()
                stores.append(store)
    for store in stores:
        store.wait()


def factor_and_basis(gram, owned, total_rows):
    size, width = owned.shape
    return pl.pallas_call(
        functools.partial(factor_kernel, root=math.sqrt(total_rows)),
        out_shape=(
            jax.ShapeDtypeStruct((size, size), jnp.float32),
            jax.ShapeDtypeStruct((size, width), jnp.float32),
        ),
        in_specs=[pl.BlockSpec(memory_space=pltpu.VMEM), pl.BlockSpec(memory_space=pl.ANY)],
        out_specs=(pl.BlockSpec(memory_space=pltpu.VMEM), pl.BlockSpec(memory_space=pl.ANY)),
        scratch_shapes=[
            pltpu.VMEM((size, size), jnp.float32),
            pltpu.VMEM((size, size), jnp.float32),
            pltpu.VMEM((size, size), jnp.bfloat16),
            pltpu.VMEM((size, width), jnp.bfloat16),
            pltpu.VMEM((size, width), jnp.float32),
            pltpu.SemaphoreType.DMA,
            pltpu.SemaphoreType.DMA((8,)),
        ],
        compiler_params=pltpu.CompilerParams(vmem_limit_bytes=VMEM_BYTES),
        name="factor_and_basis",
    )(gram, owned)


def position():
    row, col = lax.axis_index("row"), lax.axis_index("col")
    x, y = lax.div(row, 4), lax.div(col, 2)
    return row, col, x, row - 4 * x, y, col - 2 * y


def wrap(place):
    return jnp.where(place >= 4, place - 4, place)


def each_partner(place, both, visit):
    row, col, x, z, y, core = place
    ring = [y] + [wrap(y + d) for d in range(1, 4)]
    cores = [core, 1 - core] if both else [core]

    def turn(step, carry):
        outer = lax.div(step, 4)
        from_x, from_z = wrap(x + outer), wrap(z + step - 4 * outer)
        for d in range(4):
            there_row = wrap(from_x + d) * 4 + wrap(from_z + (4 - d) % 4)
            for c, there_core in enumerate(cores):
                there = (there_row, ring[d] * 2 + there_core)
                if d or c:
                    visit(there)
                else:
                    pl.when(step > 0)(functools.partial(visit, there))
        return carry

    lax.fori_loop(0, 16, turn, 0)


def upper_tiles(size):
    return [(top, left) for top in range(0, size, TILE) for left in range(top, size, TILE)]


def exchange_kernel(
    order, snapshots_hbm, owned_hbm, total,
    snapshots, staged, arrived, owned, gram, packed, from_pair, half, parts, whole,
    fetch_sem, own_sem, store_sem, block_send, block_recv,
    pair_send, pair_recv, send_sem, recv_sem, back_send, back_recv, last_send, last_recv,
):
    place = position()
    row, col, x, z, y, core = place
    pieces, count, depth, span = staged.shape
    me = row * 8 + col
    block = snapshots.shape[2]
    each = span // block
    size = gram.shape[0]
    middle = size // 2
    chips = parts.shape[0]
    sibling = (row, 2 * y + 1 - core)
    chip = row * 4 + y

    fetch = pltpu.make_async_copy(snapshots_hbm, snapshots, fetch_sem)
    fetch.start()
    barrier = pltpu.get_barrier_semaphore()

    def greet(there):
        pl.semaphore_signal(barrier, inc=1, device_id=there, device_id_type=MESH)

    each_partner(place, True, greet)
    fetch.wait()
    own = []
    for piece in range(pieces):

        def gather(there, carry, piece=piece):
            for k in range(each):
                staged[piece, there, :, k * block : (k + 1) * block] = snapshots[
                    order[(there * pieces + piece) * each + k]
                ]
            return carry

        lax.fori_loop(0, count, gather, 0)
        if piece == 0:
            pl.semaphore_wait(barrier, count - 1)

        def send_block(there, piece=piece):
            pltpu.make_async_remote_copy(
                src_ref=staged.at[piece, there[0] * 8 + there[1]],
                dst_ref=arrived.at[piece, me],
                send_sem=block_send.at[piece],
                recv_sem=block_recv.at[piece],
                device_id=there,
                device_id_type=MESH,
            ).start()

        each_partner(place, True, send_block)
        copy = pltpu.make_async_copy(staged.at[piece, me], arrived.at[piece, me], own_sem.at[piece])
        copy.start()
        own.append(copy)

    stores = []
    for piece in range(pieces):
        own[piece].wait()
        blocks = staged.at[piece, pl.ds(0, count - 1)]
        pltpu.make_async_copy(blocks, blocks, block_recv.at[piece]).wait()
        for c in range(span // CHUNK):
            got = arrived[piece, :, :, c * CHUNK : (c + 1) * CHUNK].reshape(size, CHUNK)
            owned[:, piece * span + c * CHUNK : piece * span + (c + 1) * CHUNK] = got
            for top in (0, middle):
                product = lax.dot_general(
                    got[top : top + middle], got[top:], (((1,), (1,)), ((), ())), preferred_element_type=jnp.float32
                )
                at = slice(top, top + middle), slice(top, size)
                gram[at] = product if piece == 0 and c == 0 else gram[at] + product
        at = slice(piece * span, (piece + 1) * span)
        store = pltpu.make_async_copy(owned.at[:, at], owned_hbm.at[:, at], store_sem.at[piece])
        store.start()
        stores.append(store)

    tiles = upper_tiles(size)
    for t, (top, left) in enumerate(tiles):
        packed[t // 5, t % 5] = gram[top : top + TILE, left : left + TILE].reshape(TILE // 2, 2, TILE)
    pair = pltpu.make_async_remote_copy(
        src_ref=packed.at[1 - core],
        dst_ref=from_pair,
        send_sem=pair_send,
        recv_sem=pair_recv,
        device_id=sibling,
        device_id_type=MESH,
    )
    pair.start()
    pair.wait()
    half[...] = packed[core].reshape(half.shape) + from_pair[...].reshape(half.shape)

    def send(there):
        pltpu.make_async_remote_copy(
            src_ref=half.at[there[0] * 4 + lax.div(there[1], 2)],
            dst_ref=parts.at[chip],
            send_sem=send_sem,
            recv_sem=recv_sem,
            device_id=there,
            device_id_type=MESH,
        ).start()

    each_partner(place, False, send)
    parts[chip] = half[chip]
    others = parts.at[pl.ds(0, chips - 1)]
    pltpu.make_async_copy(others, others, send_sem).wait()
    pltpu.make_async_copy(others, others, recv_sem).wait()
    summed = parts[0]
    for k in range(1, chips):
        summed = summed + parts[k]
    whole[core, chip] = summed

    def back(there):
        pltpu.make_async_remote_copy(
            src_ref=whole.at[core, chip],
            dst_ref=whole.at[core, chip],
            send_sem=back_send,
            recv_sem=back_recv,
            device_id=there,
            device_id_type=MESH,
        ).start()

    each_partner(place, False, back)
    pltpu.make_async_copy(others, others, back_send).wait()
    pltpu.make_async_copy(others, others, back_recv).wait()
    last = pltpu.make_async_remote_copy(
        src_ref=whole.at[core],
        dst_ref=whole.at[core],
        send_sem=last_send,
        recv_sem=last_recv,
        device_id=sibling,
        device_id_type=MESH,
    )
    last.start()
    total[...] = jnp.zeros_like(total)
    last.wait()
    for t, (top, left) in enumerate(tiles):
        tile = whole[t // 5].reshape(5, TILE // 2, 2, TILE)[t % 5]
        total[top : top + TILE, left : left + TILE] = tile.reshape(TILE, TILE)
    for piece in range(pieces):
        blocks = staged.at[piece, pl.ds(0, count - 1)]
        pltpu.make_async_copy(blocks, blocks, block_send.at[piece]).wait()
        stores[piece].wait()


def exchange(snapshots, block_order, devices):
    nblocks, local_count, block_rows = snapshots.shape
    size, width = devices * local_count, nblocks * block_rows // devices
    chips = devices // 2
    landing = pltpu.VMEM((HALVES, devices, local_count, width // HALVES), snapshots.dtype)
    return pl.pallas_call(
        exchange_kernel,
        out_shape=(
            jax.ShapeDtypeStruct((size, width), snapshots.dtype),
            jax.ShapeDtypeStruct((size, size), jnp.float32),
        ),
        in_specs=[pl.BlockSpec(memory_space=pltpu.SMEM), pl.BlockSpec(memory_space=pl.ANY)],
        out_specs=(pl.BlockSpec(memory_space=pl.ANY), pl.BlockSpec(memory_space=pltpu.VMEM)),
        scratch_shapes=[
            pltpu.VMEM(snapshots.shape, snapshots.dtype),
            landing,
            landing,
            pltpu.VMEM((size, width), snapshots.dtype),
            pltpu.VMEM((size, size), jnp.float32),
            pltpu.VMEM((2, 5, TILE // 2, 2, TILE), jnp.float32),
            pltpu.VMEM((5, TILE // 2, 2, TILE), jnp.float32),
            pltpu.VMEM((chips, 5, 2, TILE), jnp.float32),
            pltpu.VMEM((chips, 5, 2, TILE), jnp.float32),
            pltpu.VMEM((2, chips, 5, 2, TILE), jnp.float32),
            pltpu.SemaphoreType.DMA,
            pltpu.SemaphoreType.DMA((HALVES,)),
            pltpu.SemaphoreType.DMA((HALVES,)),
            pltpu.SemaphoreType.DMA((HALVES,)),
            pltpu.SemaphoreType.DMA((HALVES,)),
        ]
        + [pltpu.SemaphoreType.DMA] * 8,
        compiler_params=pltpu.CompilerParams(
            collective_id=0, has_side_effects=True, vmem_limit_bytes=VMEM_BYTES
        ),
        name="exchange",
    )(block_order, snapshots)


def per_device(snapshots, block_order, devices):
    local_count, total_rows = snapshots.shape
    nblocks = block_order.shape[0]
    blocks = snapshots.reshape(local_count, nblocks, total_rows // nblocks).transpose(1, 0, 2)
    owned, summed = exchange(blocks, block_order, devices)
    return factor_and_basis(summed, owned, total_rows)


def solution(mesh):
    placed = (P(("row", "col"), None), P())
    return jax.shard_map(
        functools.partial(per_device, devices=mesh.size),
        mesh=mesh,
        in_specs=placed,
        out_specs=(P(), P(None, ("row", "col"))),
        check_vma=False,
    )
```

```python
import math, functools
import jax, jax.numpy as jnp
from jax import lax
from jax.experimental import pallas as pl
from jax.experimental.pallas import tpu as pltpu
from jax.sharding import PartitionSpec as P

TILE = 128
GROUP = 8
CHUNK = 1024
HALVES = 2
VMEM_BYTES = 56 * 2**20
MESH = pl.DeviceIdType.MESH
EXACT = lax.Precision.HIGHEST


def factor_tile(work):
    lanes = lax.broadcasted_iota(jnp.int32, (8, TILE), 1)
    subs = lax.broadcasted_iota(jnp.int32, (8, TILE), 0)
    nslab = TILE // 8
    left = [work[8 * s : 8 * s + 8, :] for s in range(nslab)]
    right = [(lanes == subs + 8 * s).astype(jnp.float32) for s in range(nslab)]
    upper_rows, inverse_rows = [], []
    for start in range(0, TILE, GROUP):
        slab, base = start // 8, start % 8
        rows = [jnp.broadcast_to(left[slab][base + k : base + k + 1, :], (8, TILE)) for k in range(GROUP)]
        sides = [jnp.broadcast_to(right[slab][base + k : base + k + 1, :], (8, TILE)) for k in range(GROUP)]
        columns = [
            [jnp.broadcast_to(left[s][:, start + k : start + k + 1], (8, TILE)) for k in range(GROUP)]
            for s in range(slab, nslab)
        ]
        corner = [
            [jnp.broadcast_to(rows[k][:, start + l : start + l + 1], (8, TILE)) if l >= k else None for l in range(GROUP)]
            for k in range(GROUP)
        ]
        for k in range(GROUP):
            root = lax.rsqrt(corner[k][k])
            rows[k] = rows[k] * root
            sides[k] = sides[k] * root
            for column in columns:
                column[k] = column[k] * root
            scaled = [corner[k][l] * root if l > k else None for l in range(GROUP)]
            for l in range(k + 1, GROUP):
                for m in range(l, GROUP):
                    corner[l][m] = corner[l][m] - scaled[l] * scaled[m]
                rows[l] = rows[l] - scaled[l] * rows[k]
                sides[l] = sides[l] - scaled[l] * sides[k]
                for column in columns:
                    column[l] = column[l] - scaled[l] * column[k]
            upper_rows.append(rows[k][:1, :])
            inverse_rows.append(sides[k][:1, :])
        first = slab + (1 if base + GROUP == 8 else 0)
        for s in range(first, nslab):
            column = columns[s - slab]
            new_left, new_right = left[s], right[s]
            for k in range(GROUP):
                new_left = new_left - column[k] * rows[k]
                new_right = new_right - column[k] * sides[k]
            left[s], right[s] = new_left, new_right
    upper = jnp.concatenate(upper_rows, axis=0)
    inverse = jnp.concatenate(inverse_rows, axis=0)
    return upper, inverse


def mul(a, b):
    return lax.dot_general(a, b, (((1,), (0,)), ((), ())), precision=EXACT, preferred_element_type=jnp.float32)


def mul_t(a, b):
    return lax.dot_general(a, b, (((0,), (0,)), ((), ())), precision=EXACT, preferred_element_type=jnp.float32)


def factor_kernel(gram, owned_hbm, factor, basis_hbm, work, side, narrow, owned, basis, owned_sem, basis_sem, *, root):
    size, width = owned.shape
    fetch = pltpu.make_async_copy(owned_hbm, owned, owned_sem)
    fetch.start()
    work[...] = gram[...]
    panels = size // TILE
    stores, waiting = [], []
    for p in range(panels):
        lo, hi = p * TILE, (p + 1) * TILE
        upper, inverse = factor_tile(work[lo:hi, lo:hi])
        rows = lax.broadcasted_iota(jnp.int32, (TILE, TILE), 0)
        lanes = lax.broadcasted_iota(jnp.int32, (TILE, TILE), 1)
        factor[lo:hi, lo:hi] = jnp.where(lanes >= rows, upper, 0.0) / root
        if p:
            factor[lo:hi, :lo] = jnp.zeros((TILE, lo), jnp.float32)
            inverse = jnp.concatenate([mul(inverse, side[lo:hi, :lo]), inverse], axis=1)
        if hi < size:
            cross = mul(inverse[:, lo:hi], work[lo:hi, hi:])
            factor[lo:hi, hi:] = cross / root
            work[hi:, hi:] = work[hi:, hi:] - mul_t(cross, cross)
            update = -mul_t(cross, inverse)
            if p:
                side[hi:, :lo] = side[hi:, :lo] + update[:, :lo]
            side[hi:, lo:hi] = update[:, lo:hi]
        narrow[lo:hi, :hi] = (inverse * root).astype(jnp.bfloat16)
        if hi < size:
            narrow[lo:hi, hi:] = jnp.zeros((TILE, size - hi), jnp.bfloat16)
        if p == 1:
            fetch.wait()
        for store in waiting:
            store.start()
        stores += waiting
        waiting = []
        if p == 0:
            continue
        first = 0 if p == 1 else lo
        for c in range(width // CHUNK):
            at = slice(c * CHUNK, (c + 1) * CHUNK)
            basis[first:hi, at] = jnp.dot(
                narrow[first:hi, :hi], owned[:hi, at], preferred_element_type=jnp.float32
            )
            store = pltpu.make_async_copy(
                basis.at[first:hi, at], basis_hbm.at[first:hi, at], basis_sem.at[p - 1, c]
            )
            if hi < size:
                waiting.append(store)
            else:
                store.start()
                stores.append(store)
    for store in stores:
        store.wait()


def factor_and_basis(gram, owned, total_rows):
    size, width = owned.shape
    return pl.pallas_call(
        functools.partial(factor_kernel, root=math.sqrt(total_rows)),
        out_shape=(
            jax.ShapeDtypeStruct((size, size), jnp.float32),
            jax.ShapeDtypeStruct((size, width), jnp.float32),
        ),
        in_specs=[pl.BlockSpec(memory_space=pltpu.VMEM), pl.BlockSpec(memory_space=pl.ANY)],
        out_specs=(pl.BlockSpec(memory_space=pltpu.VMEM), pl.BlockSpec(memory_space=pl.ANY)),
        scratch_shapes=[
            pltpu.VMEM((size, size), jnp.float32),
            pltpu.VMEM((size, size), jnp.float32),
            pltpu.VMEM((size, size), jnp.bfloat16),
            pltpu.VMEM((size, width), jnp.bfloat16),
            pltpu.VMEM((size, width), jnp.float32),
            pltpu.SemaphoreType.DMA,
            pltpu.SemaphoreType.DMA((size // TILE - 1, width // CHUNK)),
        ],
        compiler_params=pltpu.CompilerParams(vmem_limit_bytes=VMEM_BYTES),
        name="factor_and_basis",
    )(gram, owned)


def position():
    row, col = lax.axis_index("row"), lax.axis_index("col")
    x, y = lax.div(row, 4), lax.div(col, 2)
    return row, col, x, row - 4 * x, y, col - 2 * y


def wrap(place):
    return jnp.where(place >= 4, place - 4, place)


def each_partner(place, both, visit):
    row, col, x, z, y, core = place
    ring = [y] + [wrap(y + d) for d in range(1, 4)]
    cores = [core, 1 - core] if both else [core]

    def turn(step, carry):
        outer = lax.div(step, 4)
        from_x, from_z = wrap(x + outer), wrap(z + step - 4 * outer)
        for d in range(4):
            there_row = wrap(from_x + d) * 4 + wrap(from_z + (4 - d) % 4)
            for c, there_core in enumerate(cores):
                there = (there_row, ring[d] * 2 + there_core)
                if d or c:
                    visit(there)
                else:
                    pl.when(step > 0)(functools.partial(visit, there))
        return carry

    lax.fori_loop(0, 16, turn, 0)


def upper_tiles(size):
    return [(top, left) for top in range(0, size, TILE) for left in range(top, size, TILE)]


def exchange_kernel(
    order, snapshots_hbm, owned_hbm, total,
    snapshots, staged, arrived, owned, gram, packed, from_pair, half, parts, whole,
    fetch_sem, own_sem, store_sem, block_send, block_recv,
    pair_send, pair_recv, send_sem, recv_sem, back_send, back_recv, last_send, last_recv,
):
    place = position()
    row, col, x, z, y, core = place
    pieces, count, depth, span = staged.shape
    me = row * 8 + col
    block = snapshots.shape[2]
    each = span // block
    size = gram.shape[0]
    middle = size // 2
    chips = parts.shape[0]
    sibling = (row, 2 * y + 1 - core)
    chip = row * 4 + y

    fetch = pltpu.make_async_copy(snapshots_hbm, snapshots, fetch_sem)
    fetch.start()
    barrier = pltpu.get_barrier_semaphore()

    def greet(there):
        pl.semaphore_signal(barrier, inc=1, device_id=there, device_id_type=MESH)

    each_partner(place, True, greet)
    fetch.wait()
    own = []
    for piece in range(pieces):

        def gather(there, carry, piece=piece):
            for k in range(each):
                staged[piece, there, :, k * block : (k + 1) * block] = snapshots[
                    order[(there * pieces + piece) * each + k]
                ]
            return carry

        lax.fori_loop(0, count, gather, 0)
        if piece == 0:
            pl.semaphore_wait(barrier, count - 1)

        def send_block(there, piece=piece):
            pltpu.make_async_remote_copy(
                src_ref=staged.at[piece, there[0] * 8 + there[1]],
                dst_ref=arrived.at[piece, me],
                send_sem=block_send.at[piece],
                recv_sem=block_recv.at[piece],
                device_id=there,
                device_id_type=MESH,
            ).start()

        each_partner(place, True, send_block)
        copy = pltpu.make_async_copy(staged.at[piece, me], arrived.at[piece, me], own_sem.at[piece])
        copy.start()
        own.append(copy)

    stores = []
    for piece in range(pieces):
        own[piece].wait()
        blocks = staged.at[piece, pl.ds(0, count - 1)]
        pltpu.make_async_copy(blocks, blocks, block_recv.at[piece]).wait()
        for c in range(span // CHUNK):
            got = arrived[piece, :, :, c * CHUNK : (c + 1) * CHUNK].reshape(size, CHUNK)
            owned[:, piece * span + c * CHUNK : piece * span + (c + 1) * CHUNK] = got
            for top in (0, middle):
                product = lax.dot_general(
                    got[top : top + middle], got[top:], (((1,), (1,)), ((), ())), preferred_element_type=jnp.float32
                )
                at = slice(top, top + middle), slice(top, size)
                gram[at] = product if piece == 0 and c == 0 else gram[at] + product
        at = slice(piece * span, (piece + 1) * span)
        store = pltpu.make_async_copy(owned.at[:, at], owned_hbm.at[:, at], store_sem.at[piece])
        store.start()
        stores.append(store)

    tiles = upper_tiles(size)
    for t, (top, left) in enumerate(tiles):
        packed[t // 5, t % 5] = gram[top : top + TILE, left : left + TILE].reshape(TILE // 2, 2, TILE)
    pair = pltpu.make_async_remote_copy(
        src_ref=packed.at[1 - core],
        dst_ref=from_pair,
        send_sem=pair_send,
        recv_sem=pair_recv,
        device_id=sibling,
        device_id_type=MESH,
    )
    pair.start()
    pair.wait()
    half[...] = packed[core].reshape(half.shape) + from_pair[...].reshape(half.shape)

    def send(there):
        pltpu.make_async_remote_copy(
            src_ref=half.at[there[0] * 4 + lax.div(there[1], 2)],
            dst_ref=parts.at[chip],
            send_sem=send_sem,
            recv_sem=recv_sem,
            device_id=there,
            device_id_type=MESH,
        ).start()

    each_partner(place, False, send)
    parts[chip] = half[chip]
    others = parts.at[pl.ds(0, chips - 1)]
    pltpu.make_async_copy(others, others, send_sem).wait()
    pltpu.make_async_copy(others, others, recv_sem).wait()
    summed = parts[0]
    for k in range(1, chips):
        summed = summed + parts[k]
    whole[core, chip] = summed

    def back(there):
        pltpu.make_async_remote_copy(
            src_ref=whole.at[core, chip],
            dst_ref=whole.at[core, chip],
            send_sem=back_send,
            recv_sem=back_recv,
            device_id=there,
            device_id_type=MESH,
        ).start()

    each_partner(place, False, back)
    pltpu.make_async_copy(others, others, back_send).wait()
    pltpu.make_async_copy(others, others, back_recv).wait()
    last = pltpu.make_async_remote_copy(
        src_ref=whole.at[core],
        dst_ref=whole.at[core],
        send_sem=last_send,
        recv_sem=last_recv,
        device_id=sibling,
        device_id_type=MESH,
    )
    last.start()
    total[...] = jnp.zeros_like(total)
    last.wait()
    for t, (top, left) in enumerate(tiles):
        tile = whole[t // 5].reshape(5, TILE // 2, 2, TILE)[t % 5]
        total[top : top + TILE, left : left + TILE] = tile.reshape(TILE, TILE)
    for piece in range(pieces):
        blocks = staged.at[piece, pl.ds(0, count - 1)]
        pltpu.make_async_copy(blocks, blocks, block_send.at[piece]).wait()
        stores[piece].wait()


def exchange(snapshots, block_order, devices):
    nblocks, local_count, block_rows = snapshots.shape
    size, width = devices * local_count, nblocks * block_rows // devices
    chips = devices // 2
    landing = pltpu.VMEM((HALVES, devices, local_count, width // HALVES), snapshots.dtype)
    return pl.pallas_call(
        exchange_kernel,
        out_shape=(
            jax.ShapeDtypeStruct((size, width), snapshots.dtype),
            jax.ShapeDtypeStruct((size, size), jnp.float32),
        ),
        in_specs=[pl.BlockSpec(memory_space=pltpu.SMEM), pl.BlockSpec(memory_space=pl.ANY)],
        out_specs=(pl.BlockSpec(memory_space=pl.ANY), pl.BlockSpec(memory_space=pltpu.VMEM)),
        scratch_shapes=[
            pltpu.VMEM(snapshots.shape, snapshots.dtype),
            landing,
            landing,
            pltpu.VMEM((size, width), snapshots.dtype),
            pltpu.VMEM((size, size), jnp.float32),
            pltpu.VMEM((2, 5, TILE // 2, 2, TILE), jnp.float32),
            pltpu.VMEM((5, TILE // 2, 2, TILE), jnp.float32),
            pltpu.VMEM((chips, 5, 2, TILE), jnp.float32),
            pltpu.VMEM((chips, 5, 2, TILE), jnp.float32),
            pltpu.VMEM((2, chips, 5, 2, TILE), jnp.float32),
            pltpu.SemaphoreType.DMA,
            pltpu.SemaphoreType.DMA((HALVES,)),
            pltpu.SemaphoreType.DMA((HALVES,)),
            pltpu.SemaphoreType.DMA((HALVES,)),
            pltpu.SemaphoreType.DMA((HALVES,)),
        ]
        + [pltpu.SemaphoreType.DMA] * 8,
        compiler_params=pltpu.CompilerParams(
            collective_id=0, has_side_effects=True, vmem_limit_bytes=VMEM_BYTES
        ),
        name="exchange",
    )(block_order, snapshots)


def per_device(snapshots, block_order, devices):
    local_count, total_rows = snapshots.shape
    nblocks = block_order.shape[0]
    blocks = snapshots.reshape(local_count, nblocks, total_rows // nblocks).transpose(1, 0, 2)
    owned, summed = exchange(blocks, block_order, devices)
    return factor_and_basis(summed, owned, total_rows)


def solution(mesh):
    placed = (P(("row", "col"), None), P())
    return jax.shard_map(
        functools.partial(per_device, devices=mesh.size),
        mesh=mesh,
        in_specs=placed,
        out_specs=(P(), P(None, ("row", "col"))),
        check_vma=False,
    )
```
